32 devices in a mesh: gx: 8 (over z, y), gy: 4 (over x, core).
Axes of the slice: x: 2, y: 2, z: 4, core: 2. Of those that a mesh axis runs over, the one named last changes fastest.
Arguments:
- thermal_anomaly: float32 [8, 256, 2048], P(None, 'gx', 'gy'), may hold values from -6 to 6
- saltiness_anomaly: float32 [8, 256, 2048], P(None, 'gx', 'gy'), may hold values from -6 to 6
- zonal_current: float32 [8, 256, 2048], P(None, 'gx', 'gy'), may hold values from -3 to 3
- meridional_current: float32 [8, 256, 2048], P(None, 'gx', 'gy'), may hold values from -3 to 3
- vertical_diffusion: float32 [7, 256, 2048], P(None, 'gx', 'gy'), may hold values from 0.1 to 10
- submerged_layers: int32 [256, 2048], P('gx', 'gy'), may hold values from 0 to 8
- strip_position_table: int32 [16], replicated, may hold values from -1 to 11, as said below
Outputs:
- temperature_out: float32 [8, 256, 2048], P(None, 'gx', 'gy')
- salinity_out: float32 [8, 256, 2048], P(None, 'gx', 'gy')
- surface_height: float32 [256, 2048], P('gx', 'gy')
- block_height: float32 [256, 1536], P('gx', 'gy')
The draws below stay inside these ranges and needn't reach their ends.
Inputs may be any that keep to these rules, and one draw needn't show every extreme that they name: `strip_position_table`: 4 bands hold -1; the others form one run of consecutive bands holding 0, 1, ..., 11 in order, and where the run begins is drawn anew.
All inputs are finite; a program needn't handle non-finite values.
Results may differ from the reference program's by a relative error of at most 0.0003.
Values sent between devices are 32-bit elements; how exact they have to be, the bound alone decides.
A program may use at most 64 MiB of HBM per device.

```python
import math
from functools import partial
import jax
import jax.numpy as jnp
from jax import lax

DEPTH_LAYERS = 8
BY = 128
SWEEPS = 4
ZONAL_POINTS = 256
MERIDIAN_SPAN = 2048
NB = 16
NOCEAN = 12


def draw_strip_position_table(key, part):
    key = jax.random.fold_in(key, 17)
    spare_bands = NB - NOCEAN
    south_land = jax.random.randint(key, (), 0, spare_bands + 1)
    band_ids = jnp.arange(NB, dtype=jnp.int32)
    inside = (band_ids >= south_land) & (band_ids < south_land + NOCEAN)
    return jnp.where(inside, band_ids - south_land, -1).astype(jnp.int32)


def touch_ends(values, key, low, high):
    dims = values.shape
    index_at = [jax.random.randint(jax.random.fold_in(key, axis), (), 0, dims[axis]) for axis in range(len(dims))]
    values = values.at[tuple(index_at)].set(low)
    longest = dims.index(max(dims))
    index_at[longest] = (index_at[longest] + 1) % dims[longest]
    return values.at[tuple(index_at)].set(high)


def block_scale(rng, shape, split, least, largest):
    level, own = 1.0, jax.random.fold_in(rng, 6)
    for axis_at, blocks in split:
        steps = jnp.exp(jax.random.uniform(jax.random.fold_in(own, axis_at), (blocks,), jnp.float32, least / len(split), largest / len(split)))
        level = level * jnp.repeat(steps, shape[axis_at] // blocks).reshape([-1 if axis == axis_at else 1 for axis in range(len(shape))])
    return level


def centred(own_key, extent, width, most, shards=(), held_as=jnp.bfloat16):
    array = width * jax.random.normal(own_key, extent, jnp.float32)
    if shards:
        array = array * block_scale(own_key, extent, shards, -0.22, 0.18)
    return jnp.clip(array, -most, most).astype(held_as)


def setup_inputs(seed: int = 0) -> dict:
    keys = jax.random.split(jax.random.key(seed), 8)
    thermal_anomaly = centred(keys[0], (DEPTH_LAYERS, ZONAL_POINTS, MERIDIAN_SPAN), 1.0, 6.0, ((1, 8), (2, 4)), jnp.float32)
    saltiness_anomaly = centred(keys[1], (DEPTH_LAYERS, ZONAL_POINTS, MERIDIAN_SPAN), 1.0, 6.0, ((1, 8), (2, 4)), jnp.float32)
    zonal_current = centred(keys[2], (DEPTH_LAYERS, ZONAL_POINTS, MERIDIAN_SPAN), 0.5, 3.0, ((1, 8), (2, 4)), jnp.float32)
    meridional_current = centred(keys[3], (DEPTH_LAYERS, ZONAL_POINTS, MERIDIAN_SPAN), 0.5, 3.0, ((1, 8), (2, 4)), jnp.float32)
    vertical_diffusion = jnp.clip(jnp.exp(math.log(10.0) - 4.6051702 * jax.random.uniform(keys[4], (DEPTH_LAYERS - 1, ZONAL_POINTS, MERIDIAN_SPAN), jnp.float32) ** block_scale(keys[4], (DEPTH_LAYERS - 1, ZONAL_POINTS, MERIDIAN_SPAN), ((1, 8), (2, 4)), -0.2, 0.2)), 0.1, 10.0)
    submerged_layers = touch_ends(jax.random.randint(keys[5], (ZONAL_POINTS, MERIDIAN_SPAN), 0, DEPTH_LAYERS + 1), jax.random.fold_in(keys[5], 1), 0, DEPTH_LAYERS).astype(jnp.int32)
    strip_position_table = draw_strip_position_table(jax.random.fold_in(keys[7], 71), 0)
    return dict(thermal_anomaly=thermal_anomaly, saltiness_anomaly=saltiness_anomaly, zonal_current=zonal_current, meridional_current=meridional_current, vertical_diffusion=vertical_diffusion, submerged_layers=submerged_layers, strip_position_table=strip_position_table)


TIME_STEP = 0.2
MIX_HORIZ = 0.25
SALT_COEF = 0.8
HEAT_COEF = 0.6
SURFACE_TERM = 0.5
CENTER = 5.5
HALF_SPAN = 5.0


def thickness(layered_planes):
    layer_indices = jnp.arange(layered_planes, dtype=jnp.float32)
    return 2.0 * (layer_indices + 1.0) / (layered_planes * (layered_planes + 1.0))


def east_of(plane):
    return jnp.roll(plane, -1, axis=-2)


def west_of(plane):
    return jnp.roll(plane, 1, axis=-2)


def north_of(plane):
    return jnp.concatenate([plane[..., 1:], jnp.zeros_like(plane[..., :1])], axis=-1)


def south_of(plane):
    return jnp.concatenate([jnp.zeros_like(plane[..., :1]), plane[..., :-1]], axis=-1)


def lateral_share(level_data, submerged_layers):
    temp_plane, salt_plane, east_plane, north_plane, level_id = level_data
    wet_mask = (level_id < submerged_layers).astype(jnp.float32)
    tracers = jnp.stack([temp_plane, salt_plane])
    east_flux = wet_mask * east_of(wet_mask) * (east_plane * (tracers + east_of(tracers)) * 0.5 - MIX_HORIZ * (east_of(tracers) - tracers))
    north_flux = wet_mask * north_of(wet_mask) * (north_plane * (tracers + north_of(tracers)) * 0.5 - MIX_HORIZ * (north_of(tracers) - tracers))
    change = east_flux - west_of(east_flux) + north_flux - south_of(north_flux)
    return wet_mask * (tracers - TIME_STEP * change)


def column_mix(updated_tracer, coupling):
    layered_planes = len(updated_tracer)
    zeros_plane = jnp.zeros_like(coupling[0])
    below_coupling = [zeros_plane] + list(coupling)
    above_coupling = list(coupling) + [zeros_plane]
    ratios = []
    values = []
    for level_index in range(layered_planes):
        pivot_value = 1.0 + below_coupling[level_index] + above_coupling[level_index]
        right_side = updated_tracer[level_index]
        if level_index > 0:
            pivot_value = pivot_value - below_coupling[level_index] * ratios[level_index - 1]
            right_side = right_side + below_coupling[level_index] * values[level_index - 1]
        ratios.append(above_coupling[level_index] / pivot_value)
        values.append(right_side / pivot_value)
    result = [None] * layered_planes
    result[layered_planes - 1] = values[layered_planes - 1]
    for level_index in range(layered_planes - 2, -1, -1):
        result[level_index] = values[level_index] + ratios[level_index] * result[level_index + 1]
    return jnp.stack(result, axis=1)


def corner_depth(depth_field, ocean_mask):
    return (ocean_mask * east_of(ocean_mask) * north_of(ocean_mask) * north_of(east_of(ocean_mask))
            * (depth_field + east_of(depth_field) + north_of(depth_field) + north_of(east_of(depth_field))) * 0.25)


def operate(surface_field, corner, ocean_mask):
    anchor = surface_field
    along_x = east_of(surface_field)
    along_y = north_of(surface_field)
    across = north_of(along_x)
    to_anchor = corner * (0.5 * (anchor - along_x) + 0.5 * (anchor - along_y) + 0.25 * (anchor - across))
    to_along_x = corner * (0.5 * (along_x - anchor) + 0.5 * (along_x - across) + 0.25 * (along_x - along_y))
    to_along_y = corner * (0.5 * (along_y - anchor) + 0.5 * (along_y - across) + 0.25 * (along_y - along_x))
    to_across = corner * (0.5 * (across - along_x) + 0.5 * (across - along_y) + 0.25 * (across - anchor))
    spread = to_anchor + west_of(to_along_x) + south_of(to_along_y) + south_of(west_of(to_across))
    return ocean_mask * (SURFACE_TERM * surface_field + spread)


def chebyshev(source, apply_operator):
    scaled = CENTER / HALF_SPAN
    height = jnp.zeros_like(source)
    residual = source
    direction = source / CENTER
    weight_now = 1.0 / scaled
    for sweep_index in range(SWEEPS):
        height = height + direction
        residual = residual - apply_operator(direction)
        if sweep_index + 1 < SWEEPS:
            weight_next = 1.0 / (2.0 * scaled - weight_now)
            direction = weight_next * weight_now * direction + (2.0 * weight_next / HALF_SPAN) * residual
            weight_now = weight_next
    return height


def reference(thermal_anomaly, saltiness_anomaly, zonal_current, meridional_current, vertical_diffusion, submerged_layers, strip_position_table):
    layered_planes = thermal_anomaly.shape[0]
    layer_indices = jnp.arange(layered_planes, dtype=jnp.int32)
    updated_tracer = lax.map(partial(lateral_share, submerged_layers=submerged_layers), (thermal_anomaly, saltiness_anomaly, zonal_current, meridional_current, layer_indices))
    wet_mask = (layer_indices[:, None, None] < submerged_layers[None]).astype(jnp.float32)
    coupling = [TIME_STEP * vertical_diffusion[level_index] * wet_mask[level_index] * wet_mask[level_index + 1] for level_index in range(layered_planes - 1)]
    mixed_columns = column_mix([updated_tracer[level_index] for level_index in range(layered_planes)], coupling)
    thicknesses = thickness(layered_planes)
    depth_field = jnp.sum(thicknesses[:, None, None] * wet_mask, axis=0)
    forcing = jnp.sum(thicknesses[:, None, None] * (SALT_COEF * mixed_columns[1] - HEAT_COEF * mixed_columns[0]), axis=0)
    band_flags = (strip_position_table >= 0).astype(jnp.float32)
    row_flags = jnp.repeat(band_flags, BY)
    ocean_mask = (depth_field > 0.0).astype(jnp.float32) * row_flags[None, :]
    source = ocean_mask * forcing
    corner = corner_depth(depth_field, ocean_mask)
    height = chebyshev(source, lambda surface_field: operate(surface_field, corner, ocean_mask))
    band_ids = jnp.arange(NB, dtype=jnp.int32)
    first_band = jnp.sum(jnp.where(strip_position_table == 0, band_ids, 0)).astype(jnp.int32)
    top_row = first_band * BY + NOCEAN * BY - 1
    north_first = (top_row - jnp.arange(NOCEAN * BY, dtype=jnp.int32)).astype(jnp.int32)
    block_height = jnp.take(height, north_first, axis=1)
    return (mixed_columns[0], mixed_columns[1], height, block_height)
```

```python
import functools

import jax
import jax.numpy as jnp
from jax import lax
from jax.experimental import pallas as pl
from jax.experimental.pallas import tpu as pltpu
from jax.sharding import PartitionSpec as P

BY = 128
KB = 3
SWEEPS = 4
RB = KB * BY

TIME_STEP = 0.2
MIX_HORIZ = 0.25
SALT_COEF = 0.8
HEAT_COEF = 0.6
SURFACE_TERM = 0.5
CENTER = 5.5
HALF_SPAN = 5.0

MESH = pl.DeviceIdType.MESH
F32 = jnp.float32
CORNERS = ((1, 1), (1, -1), (-1, 1), (-1, -1))


def roll(x, shift, axis):
    return pltpu.roll(x, shift % x.shape[axis], axis)


def step_flux(current, here, there, mask):
    half = (TIME_STEP * 0.5) * current
    mixing = TIME_STEP * MIX_HORIZ
    low = jnp.where(mask, half + mixing, 0.0)
    high = jnp.where(mask, half - mixing, 0.0)
    return [low * h + high * t for h, t in zip(here, there)]


def reverse_lanes(x):
    lane = lax.broadcasted_iota(jnp.int32, x.shape, x.ndim - 1)
    for bit in range(7):
        s = 1 << bit
        x = jnp.where((lane & s) != 0, roll(x, s, x.ndim - 1), roll(x, -s, x.ndim - 1))
    return x


def kernel(
    nx, ny, table, t_hbm, s_hbm, u_hbm, v_hbm, k_hbm, l_hbm,
    t_out, s_out, h_out, b_out,
    tv, sv, uv, vv, kv, lv, lf, st, ss, inv, ratio,
    to_e, to_w, to_n, to_s, from_w, from_e, from_s, from_n, layer_c,
    src, src_w, src_e, src_s, src_n, src_c,
    bands, pool, height, block,
    in_sem, out_sem, send1, recv1, send2, recv2, send3, recv3,
):
    levels, nrow, nlane = t_hbm.shape
    tiles = nlane // BY
    reach = (ny + KB - 1) // KB + 1
    slots = ny + KB
    gx = lax.axis_index("gx")
    gy = lax.axis_index("gy")
    east, west = lax.rem(gx + 1, nx), lax.rem(gx + nx - 1, nx)
    north, south = lax.rem(gy + 1, ny), lax.rem(gy + ny - 1, ny)
    pick_x = {1: east, -1: west}
    pick_y = {1: north, -1: south}

    barrier = pltpu.get_barrier_semaphore()
    for x in (east, west):
        for y in (gy, north, south):
            pl.semaphore_signal(barrier, inc=1, device_id=(x, y), device_id_type=MESH)
    for hop in range(1, ny):
        pl.semaphore_signal(
            barrier, inc=1, device_id=(gx, lax.rem(gy + hop, ny)), device_id_type=MESH
        )

    loads = [
        pltpu.make_async_copy(a, b, in_sem.at[i])
        for i, (a, b) in enumerate(
            ((l_hbm, lv), (t_hbm, tv), (s_hbm, sv), (u_hbm, uv), (v_hbm, vv), (k_hbm, kv))
        )
    ]
    for copy in loads:
        copy.start()

    lane = lax.broadcasted_iota(jnp.int32, (nrow, BY), 1)
    loads[0].wait()
    lf[...] = lv[...].astype(F32)
    for copy in loads[1:5]:
        copy.wait()

    for k in range(levels):
        to_e[k : k + 1, :] = tv[k, nrow - 1 : nrow, :]
        to_e[levels + k : levels + k + 1, :] = sv[k, nrow - 1 : nrow, :]
        to_e[2 * levels + k : 2 * levels + k + 1, :] = uv[k, nrow - 1 : nrow, :]
        to_w[k : k + 1, :] = tv[k, 0:1, :]
        to_w[levels + k : levels + k + 1, :] = sv[k, 0:1, :]
    to_e[3 * levels :, :] = lf[nrow - 8 :, :]
    to_w[2 * levels :, :] = lf[:8, :]
    packed = jnp.zeros((nrow, BY), F32)
    for i, ref in enumerate((tv, sv, vv)):
        for k in range(levels):
            packed = jnp.where(lane == i * levels + k, ref[k, :, nlane - 1 : nlane], packed)
    to_n[:, :BY] = packed
    to_n[:, BY:] = lf[:, nlane - BY :]
    packed = jnp.zeros((nrow, BY), F32)
    for i, ref in enumerate((tv, sv)):
        for k in range(levels):
            packed = jnp.where(lane == i * levels + k, ref[k, :, 0:1], packed)
    to_s[:, :BY] = packed
    to_s[:, BY:] = lf[:, :BY]

    def corner_of(ref, dx, dy):
        return ref.at[
            pl.ds(nrow - 8 if dx > 0 else 0, 8), pl.ds(nlane - BY if dy > 0 else 0, BY)
        ]

    def remote(source, target, sends, recvs, i, device):
        return pltpu.make_async_remote_copy(
            src_ref=source, dst_ref=target, send_sem=sends.at[i], recv_sem=recvs.at[i],
            device_id=device, device_id_type=MESH,
        )

    pl.semaphore_wait(barrier, 6 + ny - 1)
    first = [
        remote(to_e, from_w, send1, recv1, 0, (east, gy)),
        remote(to_w, from_e, send1, recv1, 1, (west, gy)),
        remote(to_n, from_s, send1, recv1, 2, (gx, north)),
        remote(to_s, from_n, send1, recv1, 3, (gx, south)),
    ] + [
        remote(corner_of(lf, dx, dy), layer_c.at[c], send1, recv1, 4 + c, (pick_x[dx], pick_y[dy]))
        for c, (dx, dy) in enumerate(CORNERS)
    ]
    for copy in first:
        copy.start()

    layers = lf[...]
    row_id = lax.broadcasted_iota(jnp.int32, (nrow, nlane), 0)
    lane_id = lax.broadcasted_iota(jnp.int32, (nrow, nlane), 1)
    least_e = jnp.where(row_id == nrow - 1, 0.0, jnp.minimum(layers, roll(layers, -1, 0)))
    least_n = jnp.where(lane_id == nlane - 1, 0.0, jnp.minimum(layers, roll(layers, -1, 1)))
    for k in range(levels):
        wet = layers > k
        tracers = [tv[k], sv[k]]
        fe = step_flux(uv[k], tracers, [roll(c, -1, 0) for c in tracers], least_e > k)
        fn = step_flux(vv[k], tracers, [roll(c, -1, 1) for c in tracers], least_n > k)
        for ref, c, e, n in zip((st, ss), tracers, fe, fn):
            ref[k] = jnp.where(wet, c, 0.0) - (e - roll(e, 1, 0)) - (n - roll(n, 1, 1))
    loads[5].wait()
    for l in range(tiles):
        part = slice(l * BY, (l + 1) * BY)
        lay = lf[:, part]
        below = jnp.zeros((nrow, BY), F32)
        last = below
        for k in range(levels):
            pivot = 1.0 + below
            if k < levels - 1:
                above = jnp.where(lay > k + 1, TIME_STEP * kv[k, :, part], 0.0)
                kv[k, :, part] = above
                pivot = pivot + above
            if k > 0:
                pivot = pivot - below * last
            one = 1.0 / pivot
            inv[k, :, part] = one
            if k < levels - 1:
                last = above * one
                ratio[k, :, part] = last
                below = above

    for copy in first:
        copy.wait_recv()
    ends_n = jnp.where(gy == ny - 1, 0.0, 1.0).astype(F32)
    ends_s = jnp.where(gy == 0, 0.0, 1.0).astype(F32)

    level_row = lax.broadcasted_iota(jnp.int32, (levels, nlane), 0).astype(F32)
    face = step_flux(
        to_e[2 * levels : 3 * levels, :],
        [to_e[:levels, :], to_e[levels : 2 * levels, :]],
        [from_e[:levels, :], from_e[levels : 2 * levels, :]],
        jnp.minimum(lf[nrow - 1 : nrow, :], from_e[2 * levels : 2 * levels + 1, :]) > level_row,
    )
    for ref, flux in zip((st, ss), face):
        for k in range(levels):
            ref[k, nrow - 1 : nrow, :] = ref[k, nrow - 1 : nrow, :] - flux[k : k + 1, :]
    face = step_flux(
        from_w[2 * levels : 3 * levels, :],
        [from_w[:levels, :], from_w[levels : 2 * levels, :]],
        [to_w[:levels, :], to_w[levels : 2 * levels, :]],
        jnp.minimum(lf[0:1, :], from_w[3 * levels + 7 : 3 * levels + 8, :]) > level_row,
    )
    for ref, flux in zip((st, ss), face):
        for k in range(levels):
            ref[k, 0:1, :] = ref[k, 0:1, :] + flux[k : k + 1, :]
    level_lane = (lane & (levels - 1)).astype(F32)

    def lane_face(here, there, least):
        held = here[:, :BY]
        current = jnp.where(
            lane < levels, roll(held, -2 * levels, 1), roll(held, -levels, 1)
        )
        return step_flux(current, [held], [there[:, :BY]], least > level_lane)[0]

    face_n = lane_face(
        to_n, from_n, jnp.minimum(lf[:, nlane - 1 : nlane], from_n[:, BY : BY + 1] * ends_n)
    )
    face_s = lane_face(
        from_s, to_s, jnp.minimum(lf[:, 0:1], from_s[:, 2 * BY - 1 : 2 * BY] * ends_s)
    )

    thick = [2.0 * (k + 1.0) / (levels * (levels + 1.0)) for k in range(levels)]
    for l in range(tiles):
        part = slice(l * BY, (l + 1) * BY)
        forcing = jnp.zeros((nrow, BY), F32)
        for i, (ref, coef) in enumerate(((st, -HEAT_COEF), (ss, SALT_COEF))):
            values = []
            for k in range(levels):
                right = ref[k, :, part]
                col = i * levels + k
                if l == tiles - 1:
                    right = right - jnp.where(lane == BY - 1, face_n[:, col : col + 1], 0.0)
                if l == 0:
                    right = right + jnp.where(lane == 0, face_s[:, col : col + 1], 0.0)
                if k > 0:
                    right = right + kv[k - 1, :, part] * values[k - 1]
                values.append(right * inv[k, :, part])
            x = values[levels - 1]
            ref[levels - 1, :, part] = x
            forcing = forcing + (coef * thick[levels - 1]) * x
            for k in range(levels - 2, -1, -1):
                x = values[k] + ratio[k, :, part] * x
                ref[k, :, part] = x
                forcing = forcing + (coef * thick[k]) * x
        src[:, part] = forcing

    second = [
        remote(src.at[pl.ds(nrow - 8, 8), :], src_w, send2, recv2, 0, (east, gy)),
        remote(src.at[pl.ds(0, 8), :], src_e, send2, recv2, 1, (west, gy)),
        remote(src.at[:, pl.ds(nlane - BY, BY)], src_s, send2, recv2, 2, (gx, north)),
        remote(src.at[:, pl.ds(0, BY)], src_n, send2, recv2, 3, (gx, south)),
    ] + [
        remote(corner_of(src, dx, dy), src_c.at[c], send2, recv2, 4 + c, (pick_x[dx], pick_y[dy]))
        for c, (dx, dy) in enumerate(CORNERS)
    ]
    for copy in second:
        copy.start()
    out_t = pltpu.make_async_copy(st, t_out, out_sem.at[0])
    out_s = pltpu.make_async_copy(ss, s_out, out_sem.at[1])
    out_t.start()
    out_s.start()

    sub8 = lax.broadcasted_iota(jnp.int32, (8, nlane), 0) < 4
    low_r = lane < BY // 2
    corner_lane = lax.broadcasted_iota(jnp.int32, (8, BY), 1) < BY // 2
    corner_sub = lax.broadcasted_iota(jnp.int32, (8, BY), 0) < 4

    def ring(centre, e, w, n, s, ne, se, nw, sw):
        rows = jnp.where(sub8, e, w)
        columns = jnp.where(low_r, n, s)
        corner = jnp.where(
            corner_sub, jnp.where(corner_lane, ne, se), jnp.where(corner_lane, nw, sw)
        )
        return jnp.concatenate(
            [
                jnp.concatenate([centre, columns], axis=1),
                jnp.concatenate([rows, corner], axis=1),
            ],
            axis=0,
        )

    wide = ring(
        layers,
        from_e[2 * levels :, :], from_w[3 * levels :, :],
        from_n[:, BY:] * ends_n, from_s[:, BY:] * ends_s,
        layer_c[3] * ends_n, layer_c[2] * ends_s, layer_c[1] * ends_n, layer_c[0] * ends_s,
    )
    depth = wide * (wide + 1.0) * (1.0 / (levels * (levels + 1.0)))
    bands_all = tiles * ny
    base = gy * tiles

    def flag(b):
        return jnp.where(table[lax.rem(b + bands_all, bands_all)] >= 0, 1.0, 0.0).astype(F32)

    full = (nrow + 8, BY)
    outer = lax.broadcasted_iota(jnp.int32, full, 1) < BY // 2
    flags = jnp.concatenate(
        [jnp.full(full, flag(base + l), F32) for l in range(tiles)]
        + [
            jnp.where(
                outer,
                jnp.full(full, flag(base + tiles), F32),
                jnp.full(full, flag(base - 1), F32),
            )
        ],
        axis=1,
    )
    ocean = jnp.where(depth > 0.0, flags, 0.0)
    pair = ocean * roll(ocean, -1, 0)
    deep = depth + roll(depth, -1, 0)
    quarter = (pair * roll(pair, -1, 1)) * (deep + roll(deep, -1, 1)) * (0.25 * 0.25)
    around = quarter + roll(quarter, 1, 0)
    around = around + roll(around, 1, 1)
    diagonal = ocean * (SURFACE_TERM + 6.0 * around)

    def operate(e):
        b = roll(e, -1, 0)
        c = roll(e, -1, 1)
        d = roll(b, -1, 1)
        p = e + d
        q = b + c
        total = p + q
        even = quarter * (total + q)
        odd = quarter * (total + p)
        spread = even + roll(odd, 1, 0) + roll(odd + roll(even, 1, 0), 1, 1)
        return diagonal * e - ocean * spread

    for copy in second:
        copy.wait_recv()
    residual = ocean * ring(
        src[...], src_e[...], src_w[...], src_n[...], src_s[...],
        src_c[3], src_c[2], src_c[1], src_c[0],
    )
    scaled = CENTER / HALF_SPAN
    direction = residual * (1.0 / CENTER)
    weight = 1.0 / scaled
    total = direction
    for _ in range(SWEEPS - 1):
        residual = residual - operate(direction)
        following = 1.0 / (2.0 * scaled - weight)
        direction = (following * weight) * direction + (2.0 * following / HALF_SPAN) * residual
        weight = following
        total = total + direction
    height[...] = total[:nrow, :nlane]
    for i in range(tiles):
        bands[i] = total[:nrow, i * BY : (i + 1) * BY]
    out_h = pltpu.make_async_copy(height, h_out, out_sem.at[2])
    out_h.start()

    def each(act_far, act_near=None):
        for i in range(tiles):
            b = base + i
            for m in range(reach):
                u = b // KB - m
                slot = lax.rem(b, KB) + KB * m
                peer = ny - 1 - u
                fits = (u >= 0) & (u < ny) & (slot < slots)

                @pl.when(fits & (peer != gy))
                def _():
                    act_far(
                        pltpu.make_async_remote_copy(
                            src_ref=bands.at[i], dst_ref=pool.at[slot],
                            send_sem=send3.at[i, m], recv_sem=recv3.at[slot],
                            device_id=(gx, peer), device_id_type=MESH,
                        )
                    )

                if act_near is None:
                    continue

                @pl.when(fits & (peer == gy))
                def _():
                    act_near(pltpu.make_async_copy(bands.at[i], pool.at[slot], recv3.at[slot]))

    each(lambda c: c.start(), lambda c: c.start())
    start = jnp.int32(0)
    for b in range(bands_all):
        start = start + jnp.where(table[b] == 0, b, 0)
    start = jnp.minimum(start, ny)
    for slot in range(slots):
        pltpu.make_async_copy(pool.at[slot], pool.at[slot], recv3.at[slot]).wait()
    for i in range(KB):
        block[:, i * BY : (i + 1) * BY] = reverse_lanes(pool[start + (KB - 1 - i)])
    out_b = pltpu.make_async_copy(block, b_out, out_sem.at[3])
    out_b.start()
    for copy in first + second:
        copy.wait_send()
    each(lambda c: c.wait_send())
    for copy in (out_t, out_s, out_h, out_b):
        copy.wait()


def body(nx, ny, t, s, u, v, k, layers, table):
    levels, nrow, nlane = t.shape
    tiles = nlane // BY
    reach = (ny + KB - 1) // KB + 1
    cube = pltpu.VMEM((levels, nrow, nlane), F32)
    lower = pltpu.VMEM((levels - 1, nrow, nlane), F32)
    plane = pltpu.VMEM((nrow, nlane), F32)
    side_y = pltpu.VMEM((nrow, BY), F32)
    side_x = pltpu.VMEM((8, nlane), F32)
    corners = pltpu.VMEM((4, 8, BY), F32)
    wide = pltpu.VMEM((3 * levels + 8, nlane), F32)
    slim = pltpu.VMEM((2 * levels + 8, nlane), F32)
    pair = pltpu.VMEM((nrow, 2 * BY), F32)
    dma = pltpu.SemaphoreType.DMA
    anywhere = pl.BlockSpec(memory_space=pl.ANY)
    return pl.pallas_call(
        functools.partial(kernel, nx, ny),
        out_shape=(
            jax.ShapeDtypeStruct(t.shape, F32),
            jax.ShapeDtypeStruct(t.shape, F32),
            jax.ShapeDtypeStruct((nrow, nlane), F32),
            jax.ShapeDtypeStruct((nrow, RB), F32),
        ),
        in_specs=[pl.BlockSpec(memory_space=pltpu.SMEM)] + [anywhere] * 6,
        out_specs=(anywhere,) * 4,
        scratch_shapes=[
            cube, cube, cube, cube, lower, pltpu.VMEM((nrow, nlane), jnp.int32), plane,
            cube, cube, cube, lower,
            wide, slim, pair, pair, wide, slim, pair, pair, corners,
            plane, side_x, side_x, side_y, side_y, corners,
            pltpu.VMEM((tiles, nrow, BY), F32), pltpu.VMEM((ny + KB, nrow, BY), F32),
            plane, pltpu.VMEM((nrow, RB), F32),
            dma((6,)), dma((4,)), dma((8,)), dma((8,)), dma((8,)), dma((8,)),
            dma((tiles, reach)), dma((ny + KB,)),
        ],
        compiler_params=pltpu.CompilerParams(
            collective_id=0, has_side_effects=True, vmem_limit_bytes=32 * 1024 * 1024
        ),
    )(table, t, s, u, v, k, layers)


def solution(mesh):
    cube = P(None, "gx", "gy")
    plane = P("gx", "gy")
    return jax.shard_map(
        functools.partial(body, mesh.shape["gx"], mesh.shape["gy"]),
        mesh=mesh,
        in_specs=(cube,) * 5 + (plane, P()),
        out_specs=(cube, cube, plane, plane),
        check_vma=False,
    )
```

```python
import functools

import jax
import jax.numpy as jnp
from jax import lax
from jax.experimental import pallas as pl
from jax.experimental.pallas import tpu as pltpu
from jax.sharding import PartitionSpec as P

BY = 128
KB = 3
SWEEPS = 4
RB = KB * BY

TIME_STEP = 0.2
MIX_HORIZ = 0.25
SALT_COEF = 0.8
HEAT_COEF = 0.6
SURFACE_TERM = 0.5
CENTER = 5.5
HALF_SPAN = 5.0

MESH = pl.DeviceIdType.MESH
F32 = jnp.float32
CORNERS = ((1, 1), (1, -1), (-1, 1), (-1, -1))


def roll(x, shift, axis):
    return pltpu.roll(x, shift % x.shape[axis], axis)


def step_flux(current, here, there, mask):
    half = (TIME_STEP * 0.5) * current
    mixing = TIME_STEP * MIX_HORIZ
    low = jnp.where(mask, half + mixing, 0.0)
    high = jnp.where(mask, half - mixing, 0.0)
    return [low * h + high * t for h, t in zip(here, there)]


def reverse_lanes(x):
    lane = lax.broadcasted_iota(jnp.int32, x.shape, x.ndim - 1)
    for bit in range(7):
        s = 1 << bit
        x = jnp.where((lane & s) != 0, roll(x, s, x.ndim - 1), roll(x, -s, x.ndim - 1))
    return x


def kernel(
    nx, ny, table, t_hbm, s_hbm, u_hbm, v_hbm, k_hbm, l_hbm,
    st, ss, height, block,
    tv, sv, uv, vv, kv, lv, lf, inv, ratio,
    to_e, to_w, to_n, to_s, from_w, from_e, from_s, from_n, layer_c,
    src, src_w, src_e, src_s, src_n, src_c,
    bands, pool,
    in_sem, send1, recv1, send2, recv2, send3, recv3,
):
    levels, nrow, nlane = t_hbm.shape
    tiles = nlane // BY
    reach = (ny + KB - 1) // KB + 1
    slots = ny + KB
    gx = lax.axis_index("gx")
    gy = lax.axis_index("gy")
    east, west = lax.rem(gx + 1, nx), lax.rem(gx + nx - 1, nx)
    north, south = lax.rem(gy + 1, ny), lax.rem(gy + ny - 1, ny)
    pick_x = {1: east, -1: west}
    pick_y = {1: north, -1: south}

    barrier = pltpu.get_barrier_semaphore()
    for x in (east, west):
        for y in (gy, north, south):
            pl.semaphore_signal(barrier, inc=1, device_id=(x, y), device_id_type=MESH)
    for hop in range(1, ny):
        pl.semaphore_signal(
            barrier, inc=1, device_id=(gx, lax.rem(gy + hop, ny)), device_id_type=MESH
        )

    loads = [
        pltpu.make_async_copy(a, b, in_sem.at[i])
        for i, (a, b) in enumerate(
            ((l_hbm, lv), (t_hbm, tv), (s_hbm, sv), (u_hbm, uv), (v_hbm, vv), (k_hbm, kv))
        )
    ]
    for copy in loads:
        copy.start()

    lane = lax.broadcasted_iota(jnp.int32, (nrow, BY), 1)
    loads[0].wait()
    lf[...] = lv[...].astype(F32)
    for copy in loads[1:5]:
        copy.wait()


    for k in range(levels):
        to_e[k : k + 1, :] = tv[k, nrow - 1 : nrow, :]
        to_e[levels + k : levels + k + 1, :] = sv[k, nrow - 1 : nrow, :]
        to_e[2 * levels + k : 2 * levels + k + 1, :] = uv[k, nrow - 1 : nrow, :]
        to_w[k : k + 1, :] = tv[k, 0:1, :]
        to_w[levels + k : levels + k + 1, :] = sv[k, 0:1, :]
    to_e[3 * levels :, :] = lf[nrow - 8 :, :]
    to_w[2 * levels :, :] = lf[:8, :]
    packed = jnp.zeros((nrow, BY), F32)
    for i, ref in enumerate((tv, sv, vv)):
        for k in range(levels):
            packed = jnp.where(lane == i * levels + k, ref[k, :, nlane - 1 : nlane], packed)
    to_n[:, :BY] = packed
    to_n[:, BY:] = lf[:, nlane - BY :]
    packed = jnp.zeros((nrow, BY), F32)
    for i, ref in enumerate((tv, sv)):
        for k in range(levels):
            packed = jnp.where(lane == i * levels + k, ref[k, :, 0:1], packed)
    to_s[:, :BY] = packed
    to_s[:, BY:] = lf[:, :BY]

    def corner_of(ref, dx, dy):
        return ref.at[
            pl.ds(nrow - 8 if dx > 0 else 0, 8), pl.ds(nlane - BY if dy > 0 else 0, BY)
        ]

    def remote(source, target, sends, recvs, i, device):
        return pltpu.make_async_remote_copy(
            src_ref=source, dst_ref=target, send_sem=sends.at[i], recv_sem=recvs.at[i],
            device_id=device, device_id_type=MESH,
        )

    pl.semaphore_wait(barrier, 6 + ny - 1)
    first = [
        remote(to_e, from_w, send1, recv1, 0, (east, gy)),
        remote(to_w, from_e, send1, recv1, 1, (west, gy)),
        remote(to_n, from_s, send1, recv1, 2, (gx, north)),
        remote(to_s, from_n, send1, recv1, 3, (gx, south)),
    ] + [
        remote(corner_of(lf, dx, dy), layer_c.at[c], send1, recv1, 4 + c, (pick_x[dx], pick_y[dy]))
        for c, (dx, dy) in enumerate(CORNERS)
    ]
    for copy in first:
        copy.start()


    layers = lf[...]
    row_id = lax.broadcasted_iota(jnp.int32, (nrow, nlane), 0)
    lane_id = lax.broadcasted_iota(jnp.int32, (nrow, nlane), 1)
    least_e = jnp.where(row_id == nrow - 1, 0.0, jnp.minimum(layers, roll(layers, -1, 0)))
    least_n = jnp.where(lane_id == nlane - 1, 0.0, jnp.minimum(layers, roll(layers, -1, 1)))
    for k in range(levels):
        wet = layers > k
        tracers = [tv[k], sv[k]]
        fe = step_flux(uv[k], tracers, [roll(c, -1, 0) for c in tracers], least_e > k)
        fn = step_flux(vv[k], tracers, [roll(c, -1, 1) for c in tracers], least_n > k)
        for ref, c, e, n in zip((st, ss), tracers, fe, fn):
            ref[k] = jnp.where(wet, c, 0.0) - (e - roll(e, 1, 0)) - (n - roll(n, 1, 1))
    loads[5].wait()
    for l in range(tiles):
        part = slice(l * BY, (l + 1) * BY)
        lay = lf[:, part]
        below = jnp.zeros((nrow, BY), F32)
        last = below
        for k in range(levels):
            pivot = 1.0 + below
            if k < levels - 1:
                above = jnp.where(lay > k + 1, TIME_STEP * kv[k, :, part], 0.0)
                kv[k, :, part] = above
                pivot = pivot + above
            if k > 0:
                pivot = pivot - below * last
            one = 1.0 / pivot
            inv[k, :, part] = one
            if k < levels - 1:
                last = above * one
                ratio[k, :, part] = last
                below = above

    for copy in first[:4]:
        copy.wait_recv()

    ends_n = jnp.where(gy == ny - 1, 0.0, 1.0).astype(F32)
    ends_s = jnp.where(gy == 0, 0.0, 1.0).astype(F32)

    level_row = lax.broadcasted_iota(jnp.int32, (levels, nlane), 0).astype(F32)
    face = step_flux(
        to_e[2 * levels : 3 * levels, :],
        [to_e[:levels, :], to_e[levels : 2 * levels, :]],
        [from_e[:levels, :], from_e[levels : 2 * levels, :]],
        jnp.minimum(lf[nrow - 1 : nrow, :], from_e[2 * levels : 2 * levels + 1, :]) > level_row,
    )
    for ref, flux in zip((st, ss), face):
        for k in range(levels):
            ref[k, nrow - 1 : nrow, :] = ref[k, nrow - 1 : nrow, :] - flux[k : k + 1, :]
    face = step_flux(
        from_w[2 * levels : 3 * levels, :],
        [from_w[:levels, :], from_w[levels : 2 * levels, :]],
        [to_w[:levels, :], to_w[levels : 2 * levels, :]],
        jnp.minimum(lf[0:1, :], from_w[3 * levels + 7 : 3 * levels + 8, :]) > level_row,
    )
    for ref, flux in zip((st, ss), face):
        for k in range(levels):
            ref[k, 0:1, :] = ref[k, 0:1, :] + flux[k : k + 1, :]
    level_lane = (lane & (levels - 1)).astype(F32)

    def lane_face(here, there, least):
        held = here[:, :BY]
        current = jnp.where(
            lane < levels, roll(held, -2 * levels, 1), roll(held, -levels, 1)
        )
        return step_flux(current, [held], [there[:, :BY]], least > level_lane)[0]

    face_n = lane_face(
        to_n, from_n, jnp.minimum(lf[:, nlane - 1 : nlane], from_n[:, BY : BY + 1] * ends_n)
    )
    face_s = lane_face(
        from_s, to_s, jnp.minimum(lf[:, 0:1], from_s[:, 2 * BY - 1 : 2 * BY] * ends_s)
    )

    thick = [2.0 * (k + 1.0) / (levels * (levels + 1.0)) for k in range(levels)]
    for l in range(tiles):
        part = slice(l * BY, (l + 1) * BY)
        forcing = jnp.zeros((nrow, BY), F32)
        for i, (ref, coef) in enumerate(((st, -HEAT_COEF), (ss, SALT_COEF))):
            values = []
            for k in range(levels):
                right = ref[k, :, part]
                col = i * levels + k
                if l == tiles - 1:
                    right = right - jnp.where(lane == BY - 1, face_n[:, col : col + 1], 0.0)
                if l == 0:
                    right = right + jnp.where(lane == 0, face_s[:, col : col + 1], 0.0)
                if k > 0:
                    right = right + kv[k - 1, :, part] * values[k - 1]
                values.append(right * inv[k, :, part])
            x = values[levels - 1]
            ref[levels - 1, :, part] = x
            forcing = forcing + (coef * thick[levels - 1]) * x
            for k in range(levels - 2, -1, -1):
                x = values[k] + ratio[k, :, part] * x
                ref[k, :, part] = x
                forcing = forcing + (coef * thick[k]) * x
        src[:, part] = forcing


    second = [
        remote(src.at[pl.ds(nrow - 8, 8), :], src_w, send2, recv2, 0, (east, gy)),
        remote(src.at[pl.ds(0, 8), :], src_e, send2, recv2, 1, (west, gy)),
        remote(src.at[:, pl.ds(nlane - BY, BY)], src_s, send2, recv2, 2, (gx, north)),
        remote(src.at[:, pl.ds(0, BY)], src_n, send2, recv2, 3, (gx, south)),
    ] + [
        remote(corner_of(src, dx, dy), src_c.at[c], send2, recv2, 4 + c, (pick_x[dx], pick_y[dy]))
        for c, (dx, dy) in enumerate(CORNERS)
    ]
    for copy in second:
        copy.start()

    sub8 = lax.broadcasted_iota(jnp.int32, (8, nlane), 0) < 4
    low_r = lane < BY // 2
    corner_lane = lax.broadcasted_iota(jnp.int32, (8, BY), 1) < BY // 2
    corner_sub = lax.broadcasted_iota(jnp.int32, (8, BY), 0) < 4

    def ring(centre, e, w, n, s, ne, se, nw, sw):
        rows = jnp.where(sub8, e, w)
        columns = jnp.where(low_r, n, s)
        corner = jnp.where(
            corner_sub, jnp.where(corner_lane, ne, se), jnp.where(corner_lane, nw, sw)
        )
        return jnp.concatenate(
            [
                jnp.concatenate([centre, columns], axis=1),
                jnp.concatenate([rows, corner], axis=1),
            ],
            axis=0,
        )

    for copy in first[4:]:
        copy.wait_recv()
    wide = ring(
        layers,
        from_e[2 * levels :, :], from_w[3 * levels :, :],
        from_n[:, BY:] * ends_n, from_s[:, BY:] * ends_s,
        layer_c[3] * ends_n, layer_c[2] * ends_s, layer_c[1] * ends_n, layer_c[0] * ends_s,
    )
    depth = wide * (wide + 1.0) * (1.0 / (levels * (levels + 1.0)))
    bands_all = tiles * ny
    base = gy * tiles

    def flag(b):
        return jnp.where(table[lax.rem(b + bands_all, bands_all)] >= 0, 1.0, 0.0).astype(F32)

    full = (nrow + 8, BY)
    outer = lax.broadcasted_iota(jnp.int32, full, 1) < BY // 2
    flags = jnp.concatenate(
        [jnp.full(full, flag(base + l), F32) for l in range(tiles)]
        + [
            jnp.where(
                outer,
                jnp.full(full, flag(base + tiles), F32),
                jnp.full(full, flag(base - 1), F32),
            )
        ],
        axis=1,
    )
    ocean = jnp.where(depth > 0.0, flags, 0.0)
    pair = ocean * roll(ocean, -1, 0)
    deep = depth + roll(depth, -1, 0)
    quarter = (pair * roll(pair, -1, 1)) * (deep + roll(deep, -1, 1)) * (0.25 * 0.25)
    around = quarter + roll(quarter, 1, 0)
    around = around + roll(around, 1, 1)
    diagonal = ocean * (SURFACE_TERM + 6.0 * around)

    def operate(e):
        b = roll(e, -1, 0)
        c = roll(e, -1, 1)
        d = roll(b, -1, 1)
        p = e + d
        q = b + c
        total = p + q
        even = quarter * (total + q)
        odd = quarter * (total + p)
        spread = even + roll(odd, 1, 0) + roll(odd + roll(even, 1, 0), 1, 1)
        return diagonal * e - ocean * spread

    for copy in second:
        copy.wait_recv()

    residual = ocean * ring(
        src[...], src_e[...], src_w[...], src_n[...], src_s[...],
        src_c[3], src_c[2], src_c[1], src_c[0],
    )
    scaled = CENTER / HALF_SPAN
    direction = residual * (1.0 / CENTER)
    weight = 1.0 / scaled
    total = direction
    for _ in range(SWEEPS - 1):
        residual = residual - operate(direction)
        following = 1.0 / (2.0 * scaled - weight)
        direction = (following * weight) * direction + (2.0 * following / HALF_SPAN) * residual
        weight = following
        total = total + direction
    height[...] = total[:nrow, :nlane]
    for i in range(tiles):
        bands[i] = total[:nrow, i * BY : (i + 1) * BY]


    def each(act_far, act_near=None):
        for i in range(tiles):
            b = base + i
            for m in range(reach):
                u = b // KB - m
                slot = lax.rem(b, KB) + KB * m
                peer = ny - 1 - u
                fits = (u >= 0) & (u < ny) & (slot < slots)

                @pl.when(fits & (peer != gy))
                def _():
                    act_far(
                        pltpu.make_async_remote_copy(
                            src_ref=bands.at[i], dst_ref=pool.at[slot],
                            send_sem=send3.at[i, m], recv_sem=recv3.at[slot],
                            device_id=(gx, peer), device_id_type=MESH,
                        )
                    )

                if act_near is None:
                    continue

                @pl.when(fits & (peer == gy))
                def _():
                    act_near(pltpu.make_async_copy(bands.at[i], pool.at[slot], recv3.at[slot]))

    each(lambda c: c.start(), lambda c: c.start())
    start = jnp.int32(0)
    for b in range(bands_all):
        start = start + jnp.where(table[b] == 0, b, 0)
    start = jnp.minimum(start, ny)
    for slot in range(slots):
        pltpu.make_async_copy(pool.at[slot], pool.at[slot], recv3.at[slot]).wait()
    for i in range(KB):
        block[:, i * BY : (i + 1) * BY] = reverse_lanes(pool[start + (KB - 1 - i)])
    for copy in first + second:
        copy.wait_send()
    each(lambda c: c.wait_send())


def write_out(*refs):
    copies = [
        pltpu.make_async_copy(refs[i], refs[4 + i], refs[8].at[i]) for i in range(4)
    ]
    for copy in copies:
        copy.start()
    for copy in copies:
        copy.wait()


def body(nx, ny, t, s, u, v, k, layers, table):
    levels, nrow, nlane = t.shape
    tiles = nlane // BY
    reach = (ny + KB - 1) // KB + 1
    cube = pltpu.VMEM((levels, nrow, nlane), F32)
    lower = pltpu.VMEM((levels - 1, nrow, nlane), F32)
    plane = pltpu.VMEM((nrow, nlane), F32)
    side_y = pltpu.VMEM((nrow, BY), F32)
    side_x = pltpu.VMEM((8, nlane), F32)
    corners = pltpu.VMEM((4, 8, BY), F32)
    wide = pltpu.VMEM((3 * levels + 8, nlane), F32)
    slim = pltpu.VMEM((2 * levels + 8, nlane), F32)
    pair = pltpu.VMEM((nrow, 2 * BY), F32)
    dma = pltpu.SemaphoreType.DMA
    anywhere = pl.BlockSpec(memory_space=pl.ANY)
    held = pl.pallas_call(
        functools.partial(kernel, nx, ny),
        out_shape=(
            pltpu.VMEM(t.shape, F32),
            pltpu.VMEM(t.shape, F32),
            pltpu.VMEM((nrow, nlane), F32),
            pltpu.VMEM((nrow, RB), F32),
        ),
        in_specs=[pl.BlockSpec(memory_space=pltpu.SMEM)] + [anywhere] * 6,
        out_specs=(pl.BlockSpec(memory_space=pltpu.VMEM),) * 4,
        scratch_shapes=[
            cube, cube, cube, cube, lower, pltpu.VMEM((nrow, nlane), jnp.int32), plane,
            cube, lower,
            wide, slim, pair, pair, wide, slim, pair, pair, corners,
            plane, side_x, side_x, side_y, side_y, corners,
            pltpu.VMEM((tiles, nrow, BY), F32), pltpu.VMEM((ny + KB, nrow, BY), F32),
            dma((6,)), dma((8,)), dma((8,)), dma((8,)), dma((8,)),
            dma((tiles, reach)), dma((ny + KB,)),
        ],
        compiler_params=pltpu.CompilerParams(
            collective_id=0, has_side_effects=True
        ),
    )(table, t, s, u, v, k, layers)
    return pl.pallas_call(
        write_out,
        out_shape=tuple(jax.ShapeDtypeStruct(x.shape, F32) for x in held),
        in_specs=[pl.BlockSpec(memory_space=pltpu.VMEM)] * 4,
        out_specs=(pl.BlockSpec(memory_space=pltpu.HBM),) * 4,
        scratch_shapes=[dma((4,))],
    )(*[pltpu.with_memory_space_constraint(x, pltpu.VMEM) for x in held])


def solution(mesh):
    cube = P(None, "gx", "gy")
    plane = P("gx", "gy")
    return jax.shard_map(
        functools.partial(body, mesh.shape["gx"], mesh.shape["gy"]),
        mesh=mesh,
        in_specs=(cube,) * 5 + (plane, P()),
        out_specs=(cube, cube, plane, plane),
        check_vma=False,
    )
```
